256 devices in a mesh: seq: 128 (over x, y, z_lo, core), kvh: 2 (over z_hi).
Axes of the slice: x: 4, y: 4, z: 8 (z_hi: 2, z_lo: 4; z = z_hi * 4 + z_lo), core: 2. Of those that a mesh axis runs over, the one named last changes fastest.
Arguments:
- queries: bfloat16 [128, 3, 4, 8, 128], P('seq', None, 'kvh'), may hold values from -125 to 125
- root_kv: bfloat16 [2, 32768, 4, 128], P(None, 'seq', 'kvh'), may hold values from -5 to 5
- doc_kv: bfloat16 [2, 32768, 4, 128], P(None, 'seq', 'kvh'), may hold values from -5 to 5
- suffix_kv: bfloat16 [2, 128, 2048, 4, 128], P(None, 'seq', None, 'kvh'), may hold values from -5 to 5
- new_kv: bfloat16 [2, 128, 3, 4, 128], P(None, 'seq', None, 'kvh'), may hold values from -5 to 5
- suffix_len: int32 [128], P('seq'), may hold values from 1 to 2048, as said below
- request_doc: int32 [128, 1], replicated, may hold values from 0 to 63; in each aligned block of 128 rows (0 to 127, 128 to 255, ...) at most 6 rows name the same one
- owner_list: int32 [128], replicated, may hold values from 0 to 127, each once
- doc_run: int32 [64], replicated, may hold values from 0 to 63, each once
Outputs:
- attended: bfloat16 [128, 3, 4096], P('seq', None, 'kvh')
The draws below stay inside these ranges and needn't reach their ends.
Inputs may be any that keep to these rules, and one draw needn't show every extreme that they name: `request_doc`: no document is the document of more than 6 requests; some document has exactly 6. `owner_list`: each request id stands in exactly one slot. `doc_run`: each run holds exactly one document. `suffix_len`: some slot has all 2048 suffix slots live.
All inputs are finite; a program needn't handle non-finite values.
Results may differ from the reference program's by a relative error of at most 0.007.
Values may be sent and summed in bfloat16 or wider, within the bound.
A program may use at most 64 MiB of HBM per device.

```python
import math
import jax
import jax.numpy as jnp
import numpy as np
from jax import lax

HD = 128
KVH = 4
GROUP = 8
STEPS = 3
SUF = 2048
REQUESTS = 128
ROOT = 32768
DOC_LEN = 512
DOCS = 64
MOST = 6


def root_base(key):
    return jnp.clip(jax.random.normal(key, (2, ROOT, KVH, HD), jnp.float32), -5.0, 5.0)


def draw_root_kv(key, part):
    base_keys = root_base(key)
    return base_keys.astype(jnp.bfloat16)


def draw_queries(key, part):
    key = jax.random.fold_in(key, 7)
    query_rows = 3.0 * jnp.clip(jax.random.normal(key, (REQUESTS, STEPS, KVH, GROUP, HD), jnp.float32), -5.0, 5.0)
    return query_rows.astype(jnp.bfloat16)


def draw_suffix_len(key, part):
    key = jax.random.fold_in(key, 5)
    length_key, spot_key = jax.random.split(key)
    lengths = jax.random.randint(length_key, (REQUESTS,), 1, SUF + 1)
    full_slot = jax.random.randint(spot_key, (), 0, REQUESTS)
    return jnp.where(jnp.arange(REQUESTS) == full_slot, SUF, lengths).astype(jnp.int32)


def steps_of(rng, extent, pieces, low, largest):
    level, own = 1.0, jax.random.fold_in(rng, 6)
    for dim, shards_of in pieces:
        steps = jnp.exp(jax.random.uniform(jax.random.fold_in(own, dim), (shards_of,), jnp.float32, low / len(pieces), largest / len(pieces)))
        level = level * jnp.repeat(steps, extent[dim] // shards_of).reshape([-1 if axis == dim else 1 for axis in range(len(extent))])
    return level


def routed_block(own_key, own, number, rows, number_of, top, limit, skew):
    sequence = jax.random.permutation(own_key, number_of)
    heavy_load, usual = load_shares(number_of, rows * top, limit, skew, True), load_shares(number_of, rows * top, limit, skew, False)
    places = jnp.arange(number_of)

    def named(sizes, offset_by):
        used = int((sizes > 0).sum())
        fixed = max(1, used // 4)
        moved = fixed + (places - fixed + offset_by * (used - fixed)) % max(1, number_of - fixed)
        return jnp.zeros((number_of,), jnp.int32).at[sequence[jnp.where(places < fixed, places, moved)]].set(jnp.asarray(sizes, jnp.int32))

    sizes = jnp.where(number % 4 == 0, named(heavy_load, number // 4), named(usual, number - number // 4 - 1))
    mixed = jax.random.permutation(jax.random.fold_in(own, 3), number_of)
    donor, taker = mixed[0:number_of // 2 * 2:2], mixed[1:number_of // 2 * 2:2]
    slack = jnp.minimum(sizes[donor] - 1, limit - sizes[taker]) // 2
    slack = jnp.where((donor == sequence[0]) | (taker == sequence[0]) | (sizes[taker] == 0), 0, jnp.maximum(slack, 0))
    moved = jax.random.randint(jax.random.fold_in(own, 4), (number_of // 2,), 0, 1 << 20) % (slack + 1)
    sizes = sizes.at[donor].add(-moved).at[taker].add(moved)
    labels = jnp.searchsorted(jnp.cumsum(sizes), jnp.arange(rows * top), side="right").astype(jnp.int32)
    listing = labels.reshape(top, rows).T
    listing = listing[jax.random.permutation(jax.random.fold_in(own, 1), rows)]
    offset_by = jax.random.randint(jax.random.fold_in(own, 2), (rows, 1), 0, top)
    return jnp.take_along_axis(listing, (jnp.arange(top)[None, :] + offset_by) % top, axis=1)


def load_shares(number_of, total, reach, lean, full):
    portions = [(1 << 20) // math.isqrt(rank ** lean) + 1 for rank in range(1, number_of + 1)]
    largest = reach if full else min(reach, max(-(-total // number_of), total * portions[0] // sum(portions)))
    least = 1 if total - largest >= number_of - 1 else 0
    given, spare = [largest] + [least] * (number_of - 1), total - largest - least * (number_of - 1)
    while spare > 0:
        movable = [i for i in range(1, number_of) if given[i] < largest] or [i for i in range(1, number_of) if given[i] < reach]
        mass, left = sum([portions[i] for i in movable]), spare
        for i in movable:
            addition = min(reach - given[i], max(1, left * portions[i] // mass), spare)
            given[i] = given[i] + addition
            spare = spare - addition
    return np.array(given)


def normal_values(stream_key, shape, deviation, reach, cuts=(), held_as=jnp.bfloat16):
    entries = jax.random.normal(stream_key, shape, jnp.float32) * deviation
    if len(cuts) > 0:
        entries = steps_of(stream_key, shape, cuts, -0.22, 0.18) * entries
    return jnp.clip(entries, min=-reach, max=reach).astype(held_as)


def setup_inputs(seed: int = 0) -> dict:
    seeds = jax.random.split(jax.random.key(seed), 10)
    queries = draw_queries(jax.random.fold_in(seeds[9], 71), 0)
    root_kv = draw_root_kv(jax.random.fold_in(seeds[9], 71), 0)
    doc_kv = normal_values(seeds[2], (2, DOCS * DOC_LEN, KVH, HD), 1.0, 5.0, ((1, 128), (2, 2)))
    suffix_kv = normal_values(seeds[3], (2, REQUESTS, SUF, KVH, HD), 1.0, 5.0, ((1, 128), (3, 2)))
    new_kv = normal_values(seeds[4], (2, REQUESTS, STEPS, KVH, HD), 1.0, 5.0, ((1, 128), (3, 2)))
    suffix_len = draw_suffix_len(jax.random.fold_in(seeds[9], 71), 0)
    request_doc_keys = jax.random.split(jax.random.fold_in(seeds[6], 1), REQUESTS // REQUESTS)
    request_doc_turns = jax.random.permutation(jax.random.fold_in(seeds[6], 3), REQUESTS // REQUESTS)
    request_doc = jax.vmap(lambda own, number: routed_block(jax.random.fold_in(seeds[6], 2), own, number, REQUESTS, DOCS, 1, MOST, 2))(request_doc_keys, request_doc_turns).reshape((REQUESTS, 1))
    owner_list = jax.random.permutation(seeds[7], REQUESTS).astype(jnp.int32)
    doc_run = jax.random.permutation(seeds[8], DOCS).astype(jnp.int32)
    return dict(queries=queries, root_kv=root_kv, doc_kv=doc_kv, suffix_kv=suffix_kv, new_kv=new_kv, suffix_len=suffix_len, request_doc=request_doc, owner_list=owner_list, doc_run=doc_run)


masked_score = -1e30


def reference(queries, root_kv, doc_kv, suffix_kv, new_kv, suffix_len, request_doc, owner_list, doc_run):
    score_scale = HD ** -0.5
    root_keys = root_kv[0].astype(jnp.float32)
    root_values = root_kv[1].astype(jnp.float32)
    slot_run = doc_run[request_doc[owner_list, 0]]
    positions = jnp.arange(SUF + STEPS, dtype=jnp.int32)
    step_ids = jnp.arange(STEPS, dtype=jnp.int32)

    def attend(inputs):
        query_rows, slot_index, length, run_index = inputs
        query_rows = query_rows.astype(jnp.float32)
        start = (run_index * DOC_LEN).astype(jnp.int32)
        doc_rows = lax.dynamic_slice_in_dim(doc_kv, start, DOC_LEN, 1).astype(jnp.float32)
        tail_rows = jnp.concatenate([suffix_kv[:, slot_index], new_kv[:, slot_index]], 1).astype(jnp.float32)
        allowed = jnp.where(positions[None, :] < SUF, positions[None, :] < length, positions[None, :] - SUF <= step_ids[:, None])
        root_scores = jnp.einsum("tkgd,nkd->tkgn", query_rows, root_keys) * score_scale
        doc_scores = jnp.einsum("tkgd,nkd->tkgn", query_rows, doc_rows[0]) * score_scale
        tail_scores = jnp.einsum("tkgd,nkd->tkgn", query_rows, tail_rows[0]) * score_scale
        tail_scores = jnp.where(allowed[:, None, None, :], tail_scores, masked_score)
        row_top = jnp.maximum(jnp.maximum(jnp.max(root_scores, -1), jnp.max(doc_scores, -1)), jnp.max(tail_scores, -1))
        numerator = jnp.zeros((STEPS, KVH, GROUP, HD), jnp.float32)
        denominator = jnp.zeros((STEPS, KVH, GROUP), jnp.float32)
        for scores, values in ((root_scores, root_values), (doc_scores, doc_rows[1]), (tail_scores, tail_rows[1])):
            rounded = lax.optimization_barrier(jnp.exp(scores - row_top[..., None]).astype(jnp.bfloat16))
            weights = rounded.astype(jnp.float32)
            numerator = numerator + jnp.einsum("tkgn,nkd->tkgd", weights, values)
            denominator = denominator + jnp.sum(weights, -1)
        result = (numerator / denominator[..., None]).astype(jnp.bfloat16)
        return result.reshape(STEPS, KVH * GROUP * HD)

    slot_ids = jnp.arange(REQUESTS, dtype=jnp.int32)
    return lax.map(attend, (queries, slot_ids, suffix_len, slot_run))
```

```python
import functools
import math

import jax
import jax.numpy as jnp
from jax import lax
from jax.experimental import pallas as pl
from jax.experimental.pallas import tpu as pltpu
from jax.sharding import PartitionSpec as P

F32 = jnp.float32
BF16 = jnp.bfloat16
HD = 128
COEF = HD ** -0.5 * math.log2(math.e)
BIG = 1e30
ROWS = 48
NT = (((1,), (1,)), ((), ()))


def lane_bcast(tile, k):
    return jnp.broadcast_to(tile[:, k : k + 1], (8, 128))


def merge_tiles(tiles):
    top = functools.reduce(jnp.maximum, tiles)
    scales = [jnp.exp2((t - top) * COEF) for t in tiles]
    total = sum(pltpu.roll(e, 64, 1) * t for e, t in zip(scales, tiles))
    lane = lax.broadcasted_iota(jnp.int32, (8, 128), 1)
    return jnp.where(lane < 64, top, total), scales


def scale_rows(scale, rows):
    n = rows.shape[0] // 8
    return jnp.concatenate([lane_bcast(scale, k) * rows[8 * k : 8 * k + 8] for k in range(n)], 0)


def kernel(
    q_hbm, root_hbm, doc_hbm, suf_hbm, new_hbm, len_hbm, rd_hbm, ol_hbm, dr_hbm,
    out_ref,
    qbuf, raw, f32s, keys, vals, suf, newb, newf, tail_s, len_s, rd_s, ol_s, dr_s,
    ns1, ss1, nr1, sr1, own2, ns2, ss2, nr2, sr2, own3, ns3, ss3, nr3, sr3,
    tail_num, tail_m, tail_l,
    lsem, kvs, kvr, zs, zr, bs, br_, as_, ar_, r1s, r1r, r2s, r2r, r3s, r3r,
):
    me = lax.axis_index("seq")
    core = lax.rem(me, 2)
    z = lax.rem(me // 2, 4)
    y = lax.rem(me // 8, 4)
    x = me // 32

    def dev(xx, yy, zz, cc):
        return {"seq": ((xx * 4 + yy) * 4 + zz) * 2 + cc}

    def zpeer(d):
        return dev(x, y, lax.rem(z + d, 4), core)

    def xpeer(d):
        return dev(lax.rem(x + d, 4), y, z, core)

    def ypeer(d):
        return dev(x, lax.rem(y + d, 4), z, core)

    apeer = (xpeer, ypeer)
    bpeer = (ypeer, xpeer)
    partner = dev(x, y, z, 1 - core)

    local = []

    def fetch(src, dst):
        c = pltpu.make_async_copy(src, dst, lsem.at[len(local)])
        c.start()
        local.append(c)
        return c

    c_q = fetch(q_hbm, qbuf.at[0, 0, 0, 0])
    c_root = fetch(root_hbm, raw.at[0, 0])
    c_doc = fetch(doc_hbm, raw.at[1, 0])
    c_ol = fetch(ol_hbm, ol_s)
    c_rd = fetch(rd_hbm, rd_s)
    c_dr = fetch(dr_hbm, dr_s)
    c_len = fetch(len_hbm, len_s)
    c_new = fetch(new_hbm, newb)
    c_suf = fetch(suf_hbm, suf)

    barrier = pltpu.get_barrier_semaphore()
    peers = [partner] + [f(d) for f in (zpeer, xpeer, ypeer) for d in (1, 2, 3)]
    for p in peers:
        pl.semaphore_signal(barrier, inc=1, device_id=p, device_id_type=pl.DeviceIdType.MESH)
    pl.semaphore_wait(barrier, len(peers))

    def send(src, dst, ss, rs, to):
        c = pltpu.make_async_remote_copy(
            src_ref=src, dst_ref=dst, send_sem=ss, recv_sem=rs,
            device_id=to, device_id_type=pl.DeviceIdType.MESH,
        )
        c.start()
        return c

    sent = []

    c_q.wait()
    for d in (1, 3, 2):
        r = 4 - d
        sent.append(send(qbuf.at[0, 0, 0, 0], qbuf.at[r // 2, 0, 0, r % 2], zs.at[d - 1], zr.at[r - 1], zpeer(d)))
    kv_root = send(root_hbm, raw.at[0, 1], kvs.at[0], kvr.at[0], partner)
    kv_doc = send(doc_hbm, raw.at[1, 1], kvs.at[1], kvr.at[1], partner)

    vals[:, :, HD:] = jnp.ones((2, 1024, HD), BF16)
    newf[...] = jnp.zeros_like(newf)

    def split_heads(src, who):
        for kv in range(2):
            f32s[src, who, kv] = raw[src, who, kv].astype(F32)
            base = src * 512 + who * 256
            for h in range(2):
                part = f32s[src, who, kv, pl.ds(h, 256, stride=2), :].astype(BF16)
                if kv == 0:
                    keys[h, base : base + 256] = part
                else:
                    vals[h, base : base + 256, :HD] = part

    c_root.wait()
    split_heads(0, 0)
    c_doc.wait()
    split_heads(1, 0)

    def wait_recv(dst, sem):
        pltpu.make_async_copy(dst, dst, sem).wait()

    for path, rels in ((0, (1,)), (1, (2, 3))):
        for r in rels:
            wait_recv(qbuf.at[r // 2, 0, 0, r % 2], zr.at[r - 1])
        for d in (1, 3, 2):
            r = 4 - d
            sent.append(send(qbuf.at[path, 0, 0], qbuf.at[path, 0, r], bs.at[path, d - 1], br_.at[path, r - 1], bpeer[path](d)))

    kv_root.wait_recv()
    split_heads(0, 1)
    kv_doc.wait_recv()
    split_heads(1, 1)

    for path in range(2):
        for r in (1, 3, 2):
            wait_recv(qbuf.at[path, 0, r], br_.at[path, r - 1])
        for d in (1, 3, 2):
            r = 4 - d
            sent.append(send(qbuf.at[path, 0], qbuf.at[path, r], as_.at[path, d - 1], ar_.at[path, r - 1], apeer[path](d)))

    for c in (c_ol, c_rd, c_dr, c_len, c_new, c_suf):
        c.wait()
    length = len_s[0]
    qown = qbuf[0, 0, 0, 0]
    row = lax.broadcasted_iota(jnp.int32, (ROWS, 1024), 0)
    col = lax.broadcasted_iota(jnp.int32, (ROWS, 1024), 1)
    same = (row // 8) % 2 == col % 2
    tops = []
    for c in range(4):
        s = lax.dot_general(qown, suf[0, 1024 * c : 1024 * c + 1024], NT, preferred_element_type=F32)
        s = jnp.where(same & (col // 2 < length - 512 * c), s, -BIG)
        tail_s[:, 1024 * c : 1024 * c + 1024] = s
        tops.append(jnp.max(s, 1, keepdims=True))
    for kv in range(2):
        for j in range(3):
            newf[kv, 2 * j : 2 * j + 2] = newb[kv, j].astype(F32)
    s_new = lax.dot_general(qown, newf[0].astype(BF16), NT, preferred_element_type=F32)
    r128, c128 = row[:, :128], col[:, :128]
    s_new = jnp.where(((r128 // 8) % 2 == c128 % 2) & (c128 // 2 <= r128 // 16) & (c128 < 6), s_new, -BIG)
    tops.append(jnp.max(s_new, 1, keepdims=True))
    top = functools.reduce(jnp.maximum, tops)
    p_new = jnp.exp2((s_new - top) * COEF).astype(BF16)
    num = lax.dot_general(p_new, newf[1].astype(BF16), (((1,), (0,)), ((), ())), preferred_element_type=F32)
    total = jnp.sum(p_new.astype(F32), 1, keepdims=True)
    for c in range(4):
        p = jnp.exp2((tail_s[:, 1024 * c : 1024 * c + 1024] - top) * COEF).astype(BF16)
        num += jnp.dot(p, suf[1, 1024 * c : 1024 * c + 1024], preferred_element_type=F32)
        total += jnp.sum(p.astype(F32), 1, keepdims=True)
    tail_num[...] = num
    tail_m[...] = jnp.broadcast_to(top, (ROWS, 128))
    tail_l[...] = jnp.broadcast_to(total, (ROWS, 128))

    lane = lax.broadcasted_iota(jnp.int32, (8, 128), 1)
    chip = me // 2

    def block(path, a_rel):
        q = qbuf[path, a_rel].reshape(8 * ROWS, HD).astype(F32).reshape(24, 2, 8, HD)
        bars = []
        for b_rel in range(4):
            for zz in range(2):
                aa, bb = (x, y) if path == 0 else (y, x)
                aa, bb = lax.rem(aa + a_rel, 4), lax.rem(bb + b_rel, 4)
                xx, yy = (aa, bb) if path == 0 else (bb, aa)
                slot = ((xx * 4 + yy) * 4 + lax.rem(z + 2 * path + zz, 4)) * 2 + core
                run = dr_s[rd_s[ol_s[slot]]]
                bars.append(jnp.full((24, 1), jnp.where(run == chip, 0.0, BIG), F32))
        bar = jnp.concatenate(bars, 0)
        nums, tile = [], jnp.zeros((8, 128), F32)
        for h in range(2):
            qh = q[:, h].reshape(24 * 8, HD).astype(BF16)
            s = lax.dot_general(qh, keys[h], NT, preferred_element_type=F32)
            s0, s1 = s[:, :512], s[:, 512:]
            m = jnp.maximum(jnp.max(s0, 1, keepdims=True), jnp.max(s1, 1, keepdims=True) - bar)
            p0 = jnp.exp2((s0 - m) * COEF).astype(BF16)
            p1 = jnp.exp2((s1 - (m + bar)) * COEF).astype(BF16)
            o = jnp.dot(p0, vals[h, :512], preferred_element_type=F32)
            o += jnp.dot(p1, vals[h, 512:], preferred_element_type=F32)
            nums.append(o[:, :HD].reshape(24, 1, 8, HD))
            for i in range(24):
                k = 2 * i + h
                tile = jnp.where(lane == k, m[8 * i : 8 * i + 8], tile)
                tile = jnp.where(lane == 64 + k, o[8 * i : 8 * i + 8, HD:], tile)
        ns1[path, a_rel] = jnp.concatenate(nums, 1).reshape(8 * ROWS, HD).astype(BF16)
        ss1[path, a_rel] = tile

    def rs1(path, d):
        r = lax.rem(4 - d, 4)
        to = apeer[path](d)
        return [
            pltpu.make_async_remote_copy(
                src_ref=ns1.at[path, d], dst_ref=nr1.at[path, r - 1], send_sem=r1s.at[path, d - 1, 0],
                recv_sem=r1r.at[path, r - 1, 0], device_id=to, device_id_type=pl.DeviceIdType.MESH),
            pltpu.make_async_remote_copy(
                src_ref=ss1.at[path, d], dst_ref=sr1.at[path, r - 1], send_sem=r1s.at[path, d - 1, 1],
                recv_sem=r1r.at[path, r - 1, 1], device_id=to, device_id_type=pl.DeviceIdType.MESH),
        ]

    def step(i, carry):
        a_rel = jnp.where(i == 2, 3, jnp.where(i == 3, 2, i))

        @pl.when(i > 0)
        def _():
            for path in range(2):
                wait_recv(qbuf.at[path, a_rel], ar_.at[path, a_rel - 1])

        for path in range(2):
            block(path, a_rel)

        @pl.when(i > 0)
        def _():
            for path in range(2):
                for c in rs1(path, a_rel):
                    c.start()

        return carry

    lax.fori_loop(0, 4, step, 0)

    for path in range(2):
        for r in (1, 3, 2):
            wait_recv(nr1.at[path, r - 1], r1r.at[path, r - 1, 0])
            wait_recv(sr1.at[path, r - 1], r1r.at[path, r - 1, 1])
        tile, scales = merge_tiles([ss1[path, 0]] + [sr1[path, r] for r in range(3)])
        acc = scale_rows(scales[0], ns1[path, 0].astype(F32))
        for r in range(3):
            acc += scale_rows(scales[r + 1], nr1[path, r].astype(F32))
        own2[path] = acc[:96]
        for d in range(3):
            ns2[path, d] = acc[96 * (d + 1) : 96 * (d + 2)].astype(BF16)
        ss2[path] = tile
        for d in (1, 3, 2):
            r = 4 - d
            sent.append(send(ns2.at[path, d - 1], nr2.at[path, r - 1], r2s.at[path, d - 1, 0], r2r.at[path, r - 1, 0], bpeer[path](d)))
            sent.append(send(ss2.at[path], sr2.at[path, r - 1], r2s.at[path, d - 1, 1], r2r.at[path, r - 1, 1], bpeer[path](d)))

    for path in (1, 0):
        for r in (1, 3, 2):
            wait_recv(nr2.at[path, r - 1], r2r.at[path, r - 1, 0])
            wait_recv(sr2.at[path, r - 1], r2r.at[path, r - 1, 1])
        tiles = [ss2[path]] + [pltpu.roll(sr2[path, r - 1], 128 - 12 * (4 - r), 1) for r in (1, 2, 3)]
        tile, scales = merge_tiles(tiles)
        acc = scale_rows(scales[0][:, :], own2[path])
        for r in range(3):
            acc += scale_rows(scales[r + 1], nr2[path, r].astype(F32))
        for zz in range(2):
            d = 2 * path + zz
            if d == 0:
                own3[...] = acc[:ROWS]
            else:
                ns3[d - 1] = acc[ROWS * zz : ROWS * zz + ROWS].astype(BF16)
        ss3[path] = tile
        for zz in (1, 0):
            d = 2 * path + zz
            if d:
                r = 4 - d
                sent.append(send(ns3.at[d - 1], nr3.at[r - 1], r3s.at[d - 1, 0], r3r.at[r - 1, 0], zpeer(d)))
                sent.append(send(ss3.at[path], sr3.at[r - 1], r3s.at[d - 1, 1], r3r.at[r - 1, 1], zpeer(d)))

    for r in (1, 2, 3):
        wait_recv(nr3.at[r - 1], r3r.at[r - 1, 0])
        wait_recv(sr3.at[r - 1], r3r.at[r - 1, 1])
    tiles = [ss3[0]]
    for r in (1, 2, 3):
        t = sr3[r - 1]
        tiles.append(pltpu.roll(t, 128 - 6, 1) if (4 - r) % 2 else t)
    parts = [(own3[...], tiles[0])] + [(nr3[r].astype(F32), tiles[r + 1]) for r in range(3)]
    for k in range(6):
        at = slice(8 * k, 8 * k + 8)
        tops = [lane_bcast(t, k) for _, t in parts] + [tail_m[at]]
        sums = [lane_bcast(t, 64 + k) for _, t in parts] + [tail_l[at]]
        vals_k = [n[at] for n, _ in parts] + [tail_num[at]]
        top = functools.reduce(jnp.maximum, tops)
        es = [jnp.exp2((t - top) * COEF) for t in tops]
        den = sum(e * s for e, s in zip(es, sums))
        num = sum(e * v for e, v in zip(es, vals_k))
        tail_num[at] = num / den
    out_ref[...] = tail_num[...].astype(BF16)

    for c in sent:
        c.wait_send()
    kv_root.wait_send()
    kv_doc.wait_send()
    for path in range(2):
        for d in (1, 2, 3):
            for c in rs1(path, d):
                c.wait_send()


def body(queries, root_kv, doc_kv, suffix_kv, new_kv, suffix_len, request_doc, owner_list, doc_run):
    vm, dma = pltpu.VMEM, pltpu.SemaphoreType.DMA
    any_spec = pl.BlockSpec(memory_space=pl.ANY)
    out = pl.pallas_call(
        kernel,
        out_shape=jax.ShapeDtypeStruct((ROWS, HD), BF16),
        in_specs=[any_spec] * 9,
        out_specs=pl.BlockSpec(memory_space=pltpu.VMEM),
        scratch_shapes=[
            vm((2, 4, 4, 2, ROWS, HD), BF16),
            vm((2, 2, 2, 512, HD), BF16),
            vm((2, 2, 2, 512, HD), F32),
            vm((2, 1024, HD), BF16),
            vm((2, 1024, 2 * HD), BF16),
            vm((2, 4096, HD), BF16),
            vm((2, 3, 2, HD), BF16),
            vm((2, 128, HD), F32),
            vm((ROWS, 4096), F32),
            pltpu.SMEM((1,), jnp.int32),
            pltpu.SMEM((128,), jnp.int32),
            pltpu.SMEM((128,), jnp.int32),
            pltpu.SMEM((64,), jnp.int32),
            vm((2, 4, 8 * ROWS, HD), BF16),
            vm((2, 4, 8, 128), F32),
            vm((2, 3, 8 * ROWS, HD), BF16),
            vm((2, 3, 8, 128), F32),
            vm((2, 96, HD), F32),
            vm((2, 3, 96, HD), BF16),
            vm((2, 8, 128), F32),
            vm((2, 3, 96, HD), BF16),
            vm((2, 3, 8, 128), F32),
            vm((ROWS, HD), F32),
            vm((3, ROWS, HD), BF16),
            vm((2, 8, 128), F32),
            vm((3, ROWS, HD), BF16),
            vm((3, 8, 128), F32),
            vm((ROWS, HD), F32),
            vm((ROWS, HD), F32),
            vm((ROWS, HD), F32),
            dma((9,)),
            dma((2,)), dma((2,)),
            dma((3,)), dma((3,)),
            dma((2, 3)), dma((2, 3)),
            dma((2, 3)), dma((2, 3)),
            dma((2, 3, 2)), dma((2, 3, 2)),
            dma((2, 3, 2)), dma((2, 3, 2)),
            dma((3, 2)), dma((3, 2)),
        ],
        compiler_params=pltpu.CompilerParams(
            collective_id=0, has_side_effects=True, vmem_limit_bytes=40 * 1024 * 1024
        ),
    )(
        queries.reshape(ROWS, HD),
        root_kv.reshape(2, 512, HD),
        doc_kv.reshape(2, 512, HD),
        suffix_kv.reshape(2, 4096, HD),
        new_kv.reshape(2, 3, 2, HD),
        suffix_len,
        request_doc.reshape(128),
        owner_list,
        doc_run,
    )
    return out.reshape(1, 3, 2048)


def solution(mesh):
    in_specs = (
        P("seq", None, "kvh", None, None),
        P(None, "seq", "kvh", None),
        P(None, "seq", "kvh", None),
        P(None, "seq", None, "kvh", None),
        P(None, "seq", None, "kvh", None),
        P("seq"),
        P(),
        P(),
        P(),
    )
    out_specs = P("seq", None, "kvh")
    return jax.shard_map(body, mesh=mesh, in_specs=in_specs, out_specs=out_specs, check_vma=False)
```

```python
import functools
import math

import jax
import jax.numpy as jnp
from jax import lax
from jax.experimental import pallas as pl
from jax.experimental.pallas import tpu as pltpu
from jax.sharding import PartitionSpec as P

F32 = jnp.float32
BF16 = jnp.bfloat16
HD = 128
COEF = HD ** -0.5 * math.log2(math.e)
BIG = 1e30
ROWS = 48
NT = (((1,), (1,)), ((), ()))


def lane_bcast(tile, k):
    return jnp.broadcast_to(tile[:, k : k + 1], (8, 128))


def merge_tiles(tiles):
    top = functools.reduce(jnp.maximum, tiles)
    scales = [jnp.exp2((t - top) * COEF) for t in tiles]
    total = sum(pltpu.roll(e, 64, 1) * t for e, t in zip(scales, tiles))
    lane = lax.broadcasted_iota(jnp.int32, (8, 128), 1)
    return jnp.where(lane < 64, top, total), scales


def pack_tile(tile):
    high = tile.astype(BF16).astype(F32)
    return jnp.concatenate([high, tile - high], 0).astype(BF16)


def unpack_tile(rows):
    rows = rows.astype(F32)
    return rows[:8] + rows[8:]


def scale_rows(scale, rows):
    n = rows.shape[0] // 8
    return jnp.concatenate([lane_bcast(scale, k) * rows[8 * k : 8 * k + 8] for k in range(n)], 0)


def kernel(
    q_hbm, root_hbm, doc_hbm, suf_hbm, new_hbm, len_hbm, rd_hbm, ol_hbm, dr_hbm,
    out_ref,
    qbuf, raw, f32s, keys, vals, suf, newb, newf, tail_s, len_s, rd_s, ol_s, dr_s,
    ns1, nr1, own2, ns2, ss2, nr2, own3, ns3, ss3, nr3,
    tail_num, tail_m, tail_l,
    lsem, kvs, kvr, zs, zr, bs, br_, as_, ar_, r1s, r1r, r2s, r2r, r3s, r3r,
):
    me = lax.axis_index("seq")
    core = lax.rem(me, 2)
    z = lax.rem(me // 2, 4)
    y = lax.rem(me // 8, 4)
    x = me // 32

    def dev(xx, yy, zz, cc):
        return {"seq": ((xx * 4 + yy) * 4 + zz) * 2 + cc}

    def zpeer(d):
        return dev(x, y, lax.rem(z + d, 4), core)

    def xpeer(d):
        return dev(lax.rem(x + d, 4), y, z, core)

    def ypeer(d):
        return dev(x, lax.rem(y + d, 4), z, core)

    apeer = (xpeer, ypeer)
    bpeer = (ypeer, xpeer)
    partner = dev(x, y, z, 1 - core)

    local = []

    def fetch(src, dst):
        c = pltpu.make_async_copy(src, dst, lsem.at[len(local)])
        c.start()
        local.append(c)
        return c

    c_q = fetch(q_hbm, qbuf.at[0, 0, 0, 0])
    c_root = fetch(root_hbm, raw.at[0, 0])
    c_doc = fetch(doc_hbm, raw.at[1, 0])
    c_ol = fetch(ol_hbm, ol_s)
    c_rd = fetch(rd_hbm, rd_s)
    c_dr = fetch(dr_hbm, dr_s)
    c_len = fetch(len_hbm, len_s)
    c_new = fetch(new_hbm, newb)
    c_suf = fetch(suf_hbm, suf)

    barrier = pltpu.get_barrier_semaphore()
    peers = [partner] + [f(d) for f in (zpeer, xpeer, ypeer) for d in (1, 2, 3)]
    for p in peers:
        pl.semaphore_signal(barrier, inc=1, device_id=p, device_id_type=pl.DeviceIdType.MESH)
    pl.semaphore_wait(barrier, len(peers))

    def send(src, dst, ss, rs, to):
        c = pltpu.make_async_remote_copy(
            src_ref=src, dst_ref=dst, send_sem=ss, recv_sem=rs,
            device_id=to, device_id_type=pl.DeviceIdType.MESH,
        )
        c.start()
        return c

    sent = []

    def to_b(path, zz):
        for d in (2, 1, 3):
            r = 4 - d
            sent.append(send(qbuf.at[path, 0, 0, zz], qbuf.at[path, 0, r, zz], bs.at[path, d - 1, zz], br_.at[path, r - 1, zz], bpeer[path](d)))

    def to_a(path, zz):
        for d in (2, 1, 3):
            r = 4 - d
            sent.append(send(qbuf.at[path, 0, 0, zz], qbuf.at[path, r, 0, zz], as_.at[path, d - 1, zz], ar_.at[path, r - 1, zz], apeer[path](d)))

    def on_to_a(path, b_rel):
        for d in (2, 1, 3):
            r = 4 - d
            sent.append(send(qbuf.at[path, 0, b_rel], qbuf.at[path, r, b_rel], as_.at[path, d - 1, b_rel + 1], ar_.at[path, r - 1, b_rel + 1], apeer[path](d)))

    def wait_recv(dst, sem):
        pltpu.make_async_copy(dst, dst, sem).wait()

    c_q.wait()
    for d in (2, 1, 3):
        r = 4 - d
        sent.append(send(qbuf.at[0, 0, 0, 0], qbuf.at[r // 2, 0, 0, r % 2], zs.at[d - 1], zr.at[r - 1], zpeer(d)))
    to_b(0, 0)
    to_a(0, 0)
    kv_root = send(root_hbm, raw.at[0, 1], kvs.at[0], kvr.at[0], partner)
    kv_doc = send(doc_hbm, raw.at[1, 1], kvs.at[1], kvr.at[1], partner)

    vals[:, :, HD:] = jnp.ones((2, 1024, HD), BF16)
    newf[...] = jnp.zeros_like(newf)

    def split_heads(src, who):
        for kv in range(2):
            f32s[src, who, kv] = raw[src, who, kv].astype(F32)
            base = src * 512 + who * 256
            for h in range(2):
                part = f32s[src, who, kv, pl.ds(h, 256, stride=2), :].astype(BF16)
                if kv == 0:
                    keys[h, base : base + 256] = part
                else:
                    vals[h, base : base + 256, :HD] = part

    c_root.wait()
    split_heads(0, 0)
    c_doc.wait()
    split_heads(1, 0)

    for r in (1, 3, 2):
        path, zz = r // 2, r % 2
        wait_recv(qbuf.at[path, 0, 0, zz], zr.at[r - 1])
        to_b(path, zz)
        to_a(path, zz)

    kv_root.wait_recv()
    split_heads(0, 1)
    kv_doc.wait_recv()
    split_heads(1, 1)

    for path in range(2):
        for r in (1, 3, 2):
            for zz in range(2):
                wait_recv(qbuf.at[path, 0, r, zz], br_.at[path, r - 1, zz])
            on_to_a(path, r)

    for c in (c_ol, c_rd, c_dr, c_len, c_new, c_suf):
        c.wait()
    length = len_s[0]
    qown = qbuf[0, 0, 0, 0]
    row = lax.broadcasted_iota(jnp.int32, (ROWS, 1024), 0)
    col = lax.broadcasted_iota(jnp.int32, (ROWS, 1024), 1)
    same = (row // 8) % 2 == col % 2
    tops = []
    for c in range(4):
        s = lax.dot_general(qown, suf[0, 1024 * c : 1024 * c + 1024], NT, preferred_element_type=F32)
        s = jnp.where(same & (col // 2 < length - 512 * c), s, -BIG)
        tail_s[:, 1024 * c : 1024 * c + 1024] = s
        tops.append(jnp.max(s, 1, keepdims=True))
    for kv in range(2):
        for j in range(3):
            newf[kv, 2 * j : 2 * j + 2] = newb[kv, j].astype(F32)
    s_new = lax.dot_general(qown, newf[0].astype(BF16), NT, preferred_element_type=F32)
    r128, c128 = row[:, :128], col[:, :128]
    s_new = jnp.where(((r128 // 8) % 2 == c128 % 2) & (c128 // 2 <= r128 // 16) & (c128 < 6), s_new, -BIG)
    tops.append(jnp.max(s_new, 1, keepdims=True))
    top = functools.reduce(jnp.maximum, tops)
    p_new = jnp.exp2((s_new - top) * COEF).astype(BF16)
    num = lax.dot_general(p_new, newf[1].astype(BF16), (((1,), (0,)), ((), ())), preferred_element_type=F32)
    total = jnp.sum(p_new.astype(F32), 1, keepdims=True)
    for c in range(4):
        p = jnp.exp2((tail_s[:, 1024 * c : 1024 * c + 1024] - top) * COEF).astype(BF16)
        num += jnp.dot(p, suf[1, 1024 * c : 1024 * c + 1024], preferred_element_type=F32)
        total += jnp.sum(p.astype(F32), 1, keepdims=True)
    tail_num[...] = num
    tail_m[...] = jnp.broadcast_to(top, (ROWS, 128))
    tail_l[...] = jnp.broadcast_to(total, (ROWS, 128))

    lane = lax.broadcasted_iota(jnp.int32, (8, 128), 1)
    chip = me // 2

    def block(path, a_rel):
        q = qbuf[path, a_rel].reshape(8 * ROWS, HD).astype(F32).reshape(24, 2, 8, HD)
        bars = []
        for b_rel in range(4):
            for zz in range(2):
                xx = lax.rem(x + jnp.where(path == 0, a_rel, b_rel), 4)
                yy = lax.rem(y + jnp.where(path == 0, b_rel, a_rel), 4)
                slot = ((xx * 4 + yy) * 4 + lax.rem(z + 2 * path + zz, 4)) * 2 + core
                run = dr_s[rd_s[ol_s[slot]]]
                bars.append(jnp.full((24, 1), jnp.where(run == chip, 0.0, BIG), F32))
        bar = jnp.concatenate(bars, 0)
        nums, tile = [], jnp.zeros((8, 128), F32)
        for h in range(2):
            qh = q[:, h].reshape(24 * 8, HD).astype(BF16)
            s = lax.dot_general(qh, keys[h], NT, preferred_element_type=F32)
            s0, s1 = s[:, :512], s[:, 512:]
            m = jnp.maximum(jnp.max(s0, 1, keepdims=True), jnp.max(s1, 1, keepdims=True) - bar)
            m = m.astype(BF16).astype(F32)
            p0 = jnp.exp2((s0 - m) * COEF).astype(BF16)
            p1 = jnp.exp2((s1 - (m + bar)) * COEF).astype(BF16)
            o = jnp.dot(p0, vals[h, :512], preferred_element_type=F32)
            o += jnp.dot(p1, vals[h, 512:], preferred_element_type=F32)
            nums.append(o[:, :HD].reshape(24, 1, 8, HD))
            for i in range(24):
                k = 2 * i + h
                tile = jnp.where(lane == k, m[8 * i : 8 * i + 8], tile)
                tile = jnp.where(lane == 64 + k, o[8 * i : 8 * i + 8, HD:], tile)
        ns1[path, a_rel, : 8 * ROWS] = jnp.concatenate(nums, 1).reshape(8 * ROWS, HD).astype(BF16)
        ns1[path, a_rel, 8 * ROWS :] = pack_tile(tile)

    def rs1(path, d):
        r = lax.rem(4 - d, 4)
        xx = lax.rem(x + jnp.where(path == 0, d, 0), 4)
        yy = lax.rem(y + jnp.where(path == 0, 0, d), 4)
        return pltpu.make_async_remote_copy(
            src_ref=ns1.at[path, d], dst_ref=nr1.at[path, r - 1], send_sem=r1s.at[path, d - 1],
            recv_sem=r1r.at[path, r - 1], device_id=dev(xx, yy, z, core), device_id_type=pl.DeviceIdType.MESH)

    def step(i, carry):
        path = jnp.where(i < 2, i, (i - 2) // 3)
        k = lax.rem(i - 2, 3)
        a_rel = jnp.where(i < 2, 0, jnp.where(k == 0, 1, 4 - k))

        @pl.when(i >= 2)
        def _():
            for zz in range(2):
                wait_recv(qbuf.at[path, a_rel, 0, zz], ar_.at[path, a_rel - 1, zz])
            for b_rel in range(1, 4):
                wait_recv(qbuf.at[path, a_rel, b_rel], ar_.at[path, a_rel - 1, b_rel + 1])

        block(path, a_rel)

        @pl.when(i >= 2)
        def _():
            rs1(path, a_rel).start()

        return carry

    lax.fori_loop(0, 8, step, 0)

    for path in range(2):
        for r in (1, 3, 2):
            wait_recv(nr1.at[path, r - 1], r1r.at[path, r - 1])
        parts = [ns1.at[path, 0]] + [nr1.at[path, r] for r in range(3)]
        tile, scales = merge_tiles([unpack_tile(p[8 * ROWS :]) for p in parts])
        acc = sum(scale_rows(e, p[: 8 * ROWS].astype(F32)) for e, p in zip(scales, parts))
        own2[path] = acc[:96]
        ss2[path] = tile
        for d in (2, 1, 3):
            r = 4 - d
            ns2[path, d - 1, :96] = acc[96 * d : 96 * (d + 1)].astype(BF16)
            ns2[path, d - 1, 96:] = pack_tile(tile)
            sent.append(send(ns2.at[path, d - 1], nr2.at[path, r - 1], r2s.at[path, d - 1], r2r.at[path, r - 1], bpeer[path](d)))

    for path in range(2):
        for r in (1, 3, 2):
            wait_recv(nr2.at[path, r - 1], r2r.at[path, r - 1])
        tiles = [ss2[path]] + [pltpu.roll(unpack_tile(nr2[path, r - 1, 96:]), 128 - 12 * (4 - r), 1) for r in (1, 2, 3)]
        tile, scales = merge_tiles(tiles)
        acc = scale_rows(scales[0], own2[path])
        for r in range(3):
            acc += scale_rows(scales[r + 1], nr2[path, r, :96].astype(F32))
        if path == 0:
            own3[...] = acc[:ROWS]
            ss3[...] = tile
        for zz in range(2):
            d = 2 * path + zz
            if d:
                r = 4 - d
                ns3[d - 1, :ROWS] = acc[ROWS * zz : ROWS * zz + ROWS].astype(BF16)
                ns3[d - 1, ROWS:] = pack_tile(tile)
                sent.append(send(ns3.at[d - 1], nr3.at[r - 1], r3s.at[d - 1], r3r.at[r - 1], zpeer(d)))

    for r in (3, 1, 2):
        wait_recv(nr3.at[r - 1], r3r.at[r - 1])
    parts = [(own3[...], ss3[...])]
    for r in (1, 2, 3):
        t = unpack_tile(nr3[r - 1, ROWS:])
        parts.append((nr3[r - 1, :ROWS].astype(F32), pltpu.roll(t, 128 - 6, 1) if r % 2 else t))
    for k in range(6):
        at = slice(8 * k, 8 * k + 8)
        tops = [lane_bcast(t, k) for _, t in parts] + [tail_m[at]]
        sums = [lane_bcast(t, 64 + k) for _, t in parts] + [tail_l[at]]
        nums = [n[at] for n, _ in parts] + [tail_num[at]]
        top = functools.reduce(jnp.maximum, tops)
        es = [jnp.exp2((t - top) * COEF) for t in tops]
        den = sum(e * s for e, s in zip(es, sums))
        res = sum(e * v for e, v in zip(es, nums)) / den
        for g in range(8):
            col = (8 * (k % 2) + g) * HD
            out_ref[0, k // 2 : k // 2 + 1, col : col + HD] = res[g : g + 1].astype(BF16)

    for c in sent:
        c.wait_send()
    kv_root.wait_send()
    kv_doc.wait_send()
    for path in range(2):
        for d in (1, 2, 3):
            rs1(path, d).wait_send()


def body(queries, root_kv, doc_kv, suffix_kv, new_kv, suffix_len, request_doc, owner_list, doc_run):
    vm, dma = pltpu.VMEM, pltpu.SemaphoreType.DMA
    any_spec = pl.BlockSpec(memory_space=pltpu.HBM)
    out = pl.pallas_call(
        kernel,
        out_shape=jax.ShapeDtypeStruct((1, 3, 2048), BF16),
        in_specs=[any_spec] * 9,
        out_specs=pl.BlockSpec(memory_space=pltpu.VMEM),
        scratch_shapes=[
            vm((2, 4, 4, 2, ROWS, HD), BF16),
            vm((2, 2, 2, 512, HD), BF16),
            vm((2, 2, 2, 512, HD), F32),
            vm((2, 1024, HD), BF16),
            vm((2, 1024, 2 * HD), BF16),
            vm((2, 4096, HD), BF16),
            vm((2, 3, 2, HD), BF16),
            vm((2, 128, HD), F32),
            vm((ROWS, 4096), F32),
            pltpu.SMEM((1,), jnp.int32),
            pltpu.SMEM((128,), jnp.int32),
            pltpu.SMEM((128,), jnp.int32),
            pltpu.SMEM((64,), jnp.int32),
            vm((2, 4, 8 * ROWS + 16, HD), BF16),
            vm((2, 3, 8 * ROWS + 16, HD), BF16),
            vm((2, 96, HD), F32),
            vm((2, 3, 112, HD), BF16),
            vm((2, 8, 128), F32),
            vm((2, 3, 112, HD), BF16),
            vm((ROWS, HD), F32),
            vm((3, 64, HD), BF16),
            vm((8, 128), F32),
            vm((3, 64, HD), BF16),
            vm((ROWS, HD), F32),
            vm((ROWS, HD), F32),
            vm((ROWS, HD), F32),
            dma((9,)),
            dma((2,)), dma((2,)),
            dma((3,)), dma((3,)),
            dma((2, 3, 2)), dma((2, 3, 2)),
            dma((2, 3, 5)), dma((2, 3, 5)),
            dma((2, 3)), dma((2, 3)),
            dma((2, 3)), dma((2, 3)),
            dma((3,)), dma((3,)),
        ],
        compiler_params=pltpu.CompilerParams(
            collective_id=0, has_side_effects=True, vmem_limit_bytes=60 * 1024 * 1024
        ),
    )(
        queries.reshape(ROWS, HD),
        root_kv.reshape(2, 512, HD),
        doc_kv.reshape(2, 512, HD),
        suffix_kv.reshape(2, 4096, HD),
        new_kv.reshape(2, 3, 2, HD),
        suffix_len,
        request_doc.reshape(128),
        owner_list,
        doc_run,
    )
    return out


def solution(mesh):
    in_specs = (
        P("seq", None, "kvh", None, None),
        P(None, "seq", "kvh", None),
        P(None, "seq", "kvh", None),
        P(None, "seq", None, "kvh", None),
        P(None, "seq", None, "kvh", None),
        P("seq"),
        P(),
        P(),
        P(),
    )
    out_specs = P("seq", None, "kvh")
    return jax.shard_map(body, mesh=mesh, in_specs=in_specs, out_specs=out_specs, check_vma=False)
```

```python
import functools
import math

import jax
import jax.numpy as jnp
from jax import lax
from jax.experimental import pallas as pl
from jax.experimental.pallas import tpu as pltpu
from jax.sharding import PartitionSpec as P

F32 = jnp.float32
BF16 = jnp.bfloat16
HD = 128
COEF = HD ** -0.5 * math.log2(math.e)
BIG = 1e30
ROWS = 48
NT = (((1,), (1,)), ((), ()))


def lane_bcast(tile, k):
    return jnp.broadcast_to(tile[:, k : k + 1], (8, 128))


def merge_tiles(tiles):
    top = functools.reduce(jnp.maximum, tiles)
    scales = [jnp.exp2((t - top) * COEF) for t in tiles]
    total = sum(pltpu.roll(e, 64, 1) * t for e, t in zip(scales, tiles))
    lane = lax.broadcasted_iota(jnp.int32, (8, 128), 1)
    return jnp.where(lane < 64, top, total), scales


def pack_tile(tile):
    high = tile.astype(BF16).astype(F32)
    return jnp.concatenate([high, tile - high], 0).astype(BF16)


def unpack_tile(rows):
    rows = rows.astype(F32)
    return rows[:8] + rows[8:]


def scale_rows(scale, rows):
    n = rows.shape[0] // 8
    return jnp.concatenate([lane_bcast(scale, k) * rows[8 * k : 8 * k + 8] for k in range(n)], 0)


def kernel(
    q_hbm, root_hbm, doc_hbm, suf_hbm, new_hbm, len_hbm, rd_hbm, ol_hbm, dr_hbm,
    out_ref,
    qbuf, raw, f32s, keys, vals, suf, newb, newf, tail_s, len_s, rd_s, ol_s, dr_s,
    ns1, nr1, own2, ss2, ns2, nr2, ns3, nr3,
    tail_num, tail_m, tail_l,
    lsem, kvs, kvr, zs, zr, bs, br_, as_, ar_, r1s, r1r, r2s, r2r, r3s, r3r,
):
    me = lax.axis_index("seq")
    core = lax.rem(me, 2)
    z = lax.rem(me // 2, 4)
    y = lax.rem(me // 8, 4)
    x = me // 32

    def dev(xx, yy, zz, cc):
        return {"seq": ((xx * 4 + yy) * 4 + zz) * 2 + cc}

    def zpeer(d, c):
        return dev(x, y, lax.rem(z + d, 4), c)

    def xpeer(d, c):
        return dev(lax.rem(x + d, 4), y, z, c)

    def ypeer(d, c):
        return dev(x, lax.rem(y + d, 4), z, c)

    def along(x_step, y_step, c):
        return dev(lax.rem(x + x_step, 4), lax.rem(y + y_step, 4), z, c)

    apeer = (xpeer, ypeer)
    bpeer = (ypeer, xpeer)
    partner = dev(x, y, z, 1 - core)

    local = []

    def fetch(src, dst):
        c = pltpu.make_async_copy(src, dst, lsem.at[len(local)])
        c.start()
        local.append(c)
        return c

    c_q = fetch(q_hbm, qbuf.at[0, 0, 0, 0])
    c_root = fetch(root_hbm, raw.at[0, 0])
    c_doc = fetch(doc_hbm, raw.at[1, 0])
    c_ol = fetch(ol_hbm, ol_s)
    c_rd = fetch(rd_hbm, rd_s)
    c_dr = fetch(dr_hbm, dr_s)
    c_len = fetch(len_hbm, len_s)
    c_new = fetch(new_hbm, newb)
    c_suf = fetch(suf_hbm, suf)

    barrier = pltpu.get_barrier_semaphore()
    axes = [(f, d) for f in (xpeer, ypeer, zpeer) for d in (1, 2, 3)]
    peers = [partner] + [f(d, c) for f, d in axes for c in (core, 1 - core)]
    for p in peers:
        pl.semaphore_signal(barrier, inc=1, device_id=p, device_id_type=pl.DeviceIdType.MESH)
    pl.semaphore_wait(barrier, len(peers))

    def send(src, dst, ss, rs, to):
        c = pltpu.make_async_remote_copy(
            src_ref=src, dst_ref=dst, send_sem=ss, recv_sem=rs,
            device_id=to, device_id_type=pl.DeviceIdType.MESH,
        )
        c.start()
        return c

    def wait_for(ref, sem):
        pltpu.make_async_copy(ref, ref, sem).wait()

    sent = []

    def to_b(path, zz):
        for d in (3, 2, 1):
            r = 4 - d
            sent.append(send(qbuf.at[path, 0, 0, zz], qbuf.at[path, 0, r, zz], bs.at[path, d - 1, zz], br_.at[path, r - 1, zz], bpeer[path](d, core)))

    def to_a(path, zz):
        for d in (3, 2, 1):
            r = 4 - d
            sent.append(send(qbuf.at[path, 0, 0, zz], qbuf.at[path, r, 0, zz], as_.at[path, d - 1, zz], ar_.at[path, r - 1, zz], apeer[path](d, core)))

    def on_to_a(path, b_rel):
        for d in (3, 2, 1):
            r = 4 - d
            sent.append(send(qbuf.at[path, 0, b_rel], qbuf.at[path, r, b_rel], as_.at[path, d - 1, b_rel + 1], ar_.at[path, r - 1, b_rel + 1], apeer[path](d, core)))

    c_q.wait()
    for d in (3, 2, 1):
        r = 4 - d
        sent.append(send(qbuf.at[0, 0, 0, 0], qbuf.at[r // 2, 0, 0, r % 2], zs.at[d - 1], zr.at[r - 1], zpeer(d, core)))
    to_b(0, 0)
    kv_root = send(root_hbm, raw.at[0, 1], kvs.at[0], kvr.at[0], partner)
    kv_doc = send(doc_hbm, raw.at[1, 1], kvs.at[1], kvr.at[1], partner)

    vals[:, :, HD:] = jnp.ones((2, 1024, HD), BF16)
    newf[...] = jnp.zeros_like(newf)

    def split_heads(src, who):
        for kv in range(2):
            f32s[src, who, kv] = raw[src, who, kv].astype(F32)
            base = src * 512 + who * 256
            for h in range(2):
                part = f32s[src, who, kv, pl.ds(h, 256, stride=2), :].astype(BF16)
                if kv == 0:
                    keys[h, base : base + 256] = part
                else:
                    vals[h, base : base + 256, :HD] = part

    c_root.wait()
    split_heads(0, 0)
    c_doc.wait()
    split_heads(1, 0)

    for r in (1, 3, 2):
        path, zz = r // 2, r % 2
        wait_for(qbuf.at[path, 0, 0, zz], zr.at[r - 1])
        to_b(path, zz)
    for path in range(2):
        for zz in range(2):
            to_a(path, zz)

    kv_root.wait_recv()
    split_heads(0, 1)
    kv_doc.wait_recv()
    split_heads(1, 1)

    for path in range(2):
        for r in (1, 3, 2):
            for zz in range(2):
                wait_for(qbuf.at[path, 0, r, zz], br_.at[path, r - 1, zz])
            on_to_a(path, r)

    for c in (c_ol, c_rd, c_dr, c_len, c_new, c_suf):
        c.wait()
    length = len_s[0]
    qown = qbuf[0, 0, 0, 0]
    row = lax.broadcasted_iota(jnp.int32, (ROWS, 1024), 0)
    col = lax.broadcasted_iota(jnp.int32, (ROWS, 1024), 1)
    same = (row // 8) % 2 == col % 2
    tops = []
    for c in range(4):
        s = lax.dot_general(qown, suf[0, 1024 * c : 1024 * c + 1024], NT, preferred_element_type=F32)
        s = jnp.where(same & (col // 2 < length - 512 * c), s, -BIG)
        tail_s[:, 1024 * c : 1024 * c + 1024] = s
        tops.append(jnp.max(s, 1, keepdims=True))
    for kv in range(2):
        for j in range(3):
            newf[kv, 2 * j : 2 * j + 2] = newb[kv, j].astype(F32)
    s_new = lax.dot_general(qown, newf[0].astype(BF16), NT, preferred_element_type=F32)
    r128, c128 = row[:, :128], col[:, :128]
    s_new = jnp.where(((r128 // 8) % 2 == c128 % 2) & (c128 // 2 <= r128 // 16) & (c128 < 6), s_new, -BIG)
    tops.append(jnp.max(s_new, 1, keepdims=True))
    top = functools.reduce(jnp.maximum, tops)
    p_new = jnp.exp2((s_new - top) * COEF).astype(BF16)
    num = lax.dot_general(p_new, newf[1].astype(BF16), (((1,), (0,)), ((), ())), preferred_element_type=F32)
    total = jnp.sum(p_new.astype(F32), 1, keepdims=True)
    for c in range(4):
        p = jnp.exp2((tail_s[:, 1024 * c : 1024 * c + 1024] - top) * COEF).astype(BF16)
        num += jnp.dot(p, suf[1, 1024 * c : 1024 * c + 1024], preferred_element_type=F32)
        total += jnp.sum(p.astype(F32), 1, keepdims=True)
    tail_num[...] = num
    tail_m[...] = jnp.broadcast_to(top, (ROWS, 128))
    tail_l[...] = jnp.broadcast_to(total, (ROWS, 128))

    lane = lax.broadcasted_iota(jnp.int32, (8, 128), 1)
    chip = me // 2

    def block(a_rel):
        q = qbuf[:, a_rel].reshape(16 * ROWS, HD).astype(F32).reshape(48, 2, 8, HD)
        bars = []
        for path in range(2):
            for b_rel in range(4):
                xx = lax.rem(x + (b_rel if path else a_rel), 4)
                yy = lax.rem(y + (a_rel if path else b_rel), 4)
                for zz in range(2):
                    slot = ((xx * 4 + yy) * 4 + lax.rem(z + 2 * path + zz, 4)) * 2 + core
                    run = dr_s[rd_s[ol_s[slot]]]
                    bars.append(jnp.full((24, 1), jnp.where(run == chip, 0.0, BIG), F32))
        bar = jnp.concatenate(bars, 0)
        nums, tiles = [], [jnp.zeros((8, 128), F32)] * 2
        for h in range(2):
            qh = q[:, h].reshape(48 * 8, HD).astype(BF16)
            s = lax.dot_general(qh, keys[h], NT, preferred_element_type=F32)
            s0, s1 = s[:, :512], s[:, 512:]
            m = jnp.maximum(jnp.max(s0, 1, keepdims=True), jnp.max(s1, 1, keepdims=True) - bar)
            m = m.astype(BF16).astype(F32)
            p0 = jnp.exp2((s0 - m) * COEF).astype(BF16)
            p1 = jnp.exp2((s1 - (m + bar)) * COEF).astype(BF16)
            o = jnp.dot(p0, vals[h, :512], preferred_element_type=F32)
            o += jnp.dot(p1, vals[h, 512:], preferred_element_type=F32)
            nums.append(o[:, :HD].reshape(48, 1, 8, HD))
            for i in range(48):
                k = 2 * (i % 24) + h
                tile = jnp.where(lane == k, m[8 * i : 8 * i + 8], tiles[i // 24])
                tiles[i // 24] = jnp.where(lane == 64 + k, o[8 * i : 8 * i + 8, HD:], tile)
        ns1[:, a_rel, : 8 * ROWS] = jnp.concatenate(nums, 1).reshape(2, 8 * ROWS, HD).astype(BF16)
        for path in range(2):
            ns1[path, a_rel, 8 * ROWS :] = pack_tile(tiles[path])

    def rs1(path, d):
        r = lax.rem(4 - d, 4)
        to = along(jnp.where(path == 0, d, 0), jnp.where(path == 0, 0, d), 1)
        return pltpu.make_async_remote_copy(
            src_ref=ns1.at[path, d], dst_ref=nr1.at[core, path, r], send_sem=r1s.at[path, d],
            recv_sem=r1r.at[core, path, r], device_id=to, device_id_type=pl.DeviceIdType.MESH)

    def step(a_rel, carry):
        @pl.when(a_rel > 0)
        def _():
            for path in range(2):
                for zz in range(2):
                    wait_for(qbuf.at[path, a_rel, 0, zz], ar_.at[path, a_rel - 1, zz])
                for b_rel in range(1, 4):
                    wait_for(qbuf.at[path, a_rel, b_rel], ar_.at[path, a_rel - 1, b_rel + 1])

        block(a_rel)

        @pl.when((a_rel > 0) | (core == 0))
        def _():
            for path in range(2):
                rs1(path, a_rel).start()

        @pl.when((a_rel == 0) & (core == 1))
        def _():
            for path in range(2):
                pltpu.make_async_copy(ns1.at[path, 0], nr1.at[1, path, 0], r1r.at[1, path, 0]).start()

        return carry

    lax.fori_loop(0, 4, step, 0)

    def rs2(plane, path, d):
        r = 4 - d
        to = along(jnp.where(path == 0, 0, d), jnp.where(path == 0, d, 0), 1)
        return pltpu.make_async_remote_copy(
            src_ref=ns2.at[plane, path, d - 1], dst_ref=nr2.at[plane, path, r - 1], send_sem=r2s.at[plane, path, d - 1],
            recv_sem=r2r.at[plane, path, r - 1], device_id=to, device_id_type=pl.DeviceIdType.MESH)

    def rs3(plane, path, zz):
        d = 2 * path + zz
        r = lax.rem(4 - d, 4)
        return pltpu.make_async_remote_copy(
            src_ref=ns3.at[plane, d], dst_ref=nr3.at[r], send_sem=r3s.at[plane, d], recv_sem=r3r.at[r],
            device_id=zpeer(d, plane), device_id_type=pl.DeviceIdType.MESH)

    def back_a(i, carry):
        plane, path = 1 - lax.rem(i, 2), i // 2
        for r in (0, 3, 2, 1):
            wait_for(nr1.at[plane, path, r], r1r.at[plane, path, r])
        msgs = [nr1.at[plane, path, r] for r in range(4)]
        tile, scales = merge_tiles([unpack_tile(p[8 * ROWS :]) for p in msgs])
        acc = sum(scale_rows(e, p[: 8 * ROWS].astype(F32)) for e, p in zip(scales, msgs))
        own2[plane, path] = acc[:96]
        ss2[plane, path] = tile
        for d in (2, 1, 3):
            ns2[plane, path, d - 1, :96] = acc[96 * d : 96 * (d + 1)].astype(BF16)
            ns2[plane, path, d - 1, 96:] = pack_tile(tile)
        for d in (2, 1, 3):
            rs2(plane, path, d).start()
        return carry

    def back_b(i, carry):
        plane, path = 1 - lax.rem(i, 2), i // 2
        for r in (1, 3, 2):
            wait_for(nr2.at[plane, path, r - 1], r2r.at[plane, path, r - 1])
        tiles = [ss2[plane, path]]
        tiles += [pltpu.roll(unpack_tile(nr2[plane, path, r - 1, 96:]), 128 - 12 * (4 - r), 1) for r in (1, 2, 3)]
        tile, scales = merge_tiles(tiles)
        acc = scale_rows(scales[0], own2[plane, path])
        for r in range(3):
            acc += scale_rows(scales[r + 1], nr2[plane, path, r, :96].astype(F32))
        for zz in range(2):
            ns3[plane, 2 * path + zz, :ROWS] = acc[ROWS * zz : ROWS * zz + ROWS].astype(BF16)
            ns3[plane, 2 * path + zz, ROWS:] = pack_tile(tile)
        here = (plane == 1) & (path == 0)

        @pl.when(jnp.logical_not(here))
        def _():
            rs3(plane, path, 0).start()

        @pl.when(here)
        def _():
            pltpu.make_async_copy(ns3.at[1, 0], nr3.at[0], r3r.at[0]).start()

        rs3(plane, path, 1).start()
        return carry

    @pl.when(core == 1)
    def _():
        lax.fori_loop(0, 4, back_a, 0)
        lax.fori_loop(0, 4, back_b, 0)

    for r in (0, 3, 1, 2):
        wait_for(nr3.at[r], r3r.at[r])
    parts = []
    for r in range(4):
        t = unpack_tile(nr3[r, ROWS:])
        parts.append((nr3[r, :ROWS].astype(F32), pltpu.roll(t, 128 - 6, 1) if r % 2 else t))
    for k in range(6):
        at = slice(8 * k, 8 * k + 8)
        tops = [lane_bcast(t, k) for _, t in parts] + [tail_m[at]]
        sums = [lane_bcast(t, 64 + k) for _, t in parts] + [tail_l[at]]
        nums = [n[at] for n, _ in parts] + [tail_num[at]]
        top = functools.reduce(jnp.maximum, tops)
        es = [jnp.exp2((t - top) * COEF) for t in tops]
        den = sum(e * s for e, s in zip(es, sums))
        res = sum(e * v for e, v in zip(es, nums)) / den
        for g in range(8):
            col = (8 * (k % 2) + g) * HD
            out_ref[0, k // 2 : k // 2 + 1, col : col + HD] = res[g : g + 1].astype(BF16)

    kv_root.wait_send()
    kv_doc.wait_send()
    for path in range(2):
        for d in (1, 2, 3):
            wait_for(ns1.at[path, d], r1s.at[path, d])

    for c in sent:
        c.wait_send()

    @pl.when(core == 0)
    def _():
        for path in range(2):
            wait_for(ns1.at[path, 0], r1s.at[path, 0])

    @pl.when(core == 1)
    def _():
        for plane in range(2):
            for path in range(2):
                for d in (1, 2, 3):
                    wait_for(ns2.at[plane, path, d - 1], r2s.at[plane, path, d - 1])
            for d in range(4):
                if (plane, d) != (1, 0):
                    wait_for(ns3.at[plane, d], r3s.at[plane, d])


def body(queries, root_kv, doc_kv, suffix_kv, new_kv, suffix_len, request_doc, owner_list, doc_run):
    vm, dma = pltpu.VMEM, pltpu.SemaphoreType.DMA
    any_spec = pl.BlockSpec(memory_space=pltpu.HBM)
    out = pl.pallas_call(
        kernel,
        out_shape=pltpu.VMEM((1, 3, 2048), BF16),
        in_specs=[any_spec] * 9,
        out_specs=pl.BlockSpec(memory_space=pltpu.VMEM),
        scratch_shapes=[
            vm((2, 4, 4, 2, ROWS, HD), BF16),
            vm((2, 2, 2, 512, HD), BF16),
            vm((2, 2, 2, 512, HD), F32),
            vm((2, 1024, HD), BF16),
            vm((2, 1024, 2 * HD), BF16),
            vm((2, 4096, HD), BF16),
            vm((2, 3, 2, HD), BF16),
            vm((2, 128, HD), F32),
            vm((ROWS, 4096), F32),
            pltpu.SMEM((1,), jnp.int32),
            pltpu.SMEM((128,), jnp.int32),
            pltpu.SMEM((128,), jnp.int32),
            pltpu.SMEM((64,), jnp.int32),
            vm((2, 4, 8 * ROWS + 16, HD), BF16),
            vm((2, 2, 4, 8 * ROWS + 16, HD), BF16),
            vm((2, 2, 96, HD), F32),
            vm((2, 2, 8, 128), F32),
            vm((2, 2, 3, 112, HD), BF16),
            vm((2, 2, 3, 112, HD), BF16),
            vm((2, 4, 64, HD), BF16),
            vm((4, 64, HD), BF16),
            vm((ROWS, HD), F32),
            vm((ROWS, HD), F32),
            vm((ROWS, HD), F32),
            dma((9,)),
            dma((2,)), dma((2,)),
            dma((3,)), dma((3,)),
            dma((2, 3, 2)), dma((2, 3, 2)),
            dma((2, 3, 5)), dma((2, 3, 5)),
            dma((2, 4)), dma((2, 2, 4)),
            dma((2, 2, 3)), dma((2, 2, 3)),
            dma((2, 4)), dma((4,)),
        ],
        compiler_params=pltpu.CompilerParams(
            collective_id=0, has_side_effects=True, vmem_limit_bytes=60 * 1024 * 1024
        ),
    )(
        queries.reshape(ROWS, HD),
        root_kv.reshape(2, 512, HD),
        doc_kv.reshape(2, 512, HD),
        suffix_kv.reshape(2, 4096, HD),
        new_kv.reshape(2, 3, 2, HD),
        suffix_len,
        request_doc.reshape(128),
        owner_list,
        doc_run,
    )
    return out


def solution(mesh):
    in_specs = (
        P("seq", None, "kvh", None, None),
        P(None, "seq", "kvh", None),
        P(None, "seq", "kvh", None),
        P(None, "seq", None, "kvh", None),
        P(None, "seq", None, "kvh", None),
        P("seq"),
        P(),
        P(),
        P(),
    )
    out_specs = P("seq", None, "kvh")
    return jax.shard_map(body, mesh=mesh, in_specs=in_specs, out_specs=out_specs, check_vma=False)
```

```python
import functools
import math

import jax
import jax.numpy as jnp
from jax import lax
from jax.experimental import pallas as pl
from jax.experimental.pallas import tpu as pltpu
from jax.sharding import PartitionSpec as P

F32 = jnp.float32
BF16 = jnp.bfloat16
HD = 128
COEF = HD ** -0.5 * math.log2(math.e)
BIG = 1e30
ROWS = 48
NT = (((1,), (1,)), ((), ()))


def lane_bcast(tile, k):
    return jnp.broadcast_to(tile[:, k : k + 1], (8, 128))


def merge_tiles(tiles):
    top = functools.reduce(jnp.maximum, tiles)
    scales = [jnp.exp2((t - top) * COEF) for t in tiles]
    total = sum(pltpu.roll(e, 64, 1) * t for e, t in zip(scales, tiles))
    lane = lax.broadcasted_iota(jnp.int32, (8, 128), 1)
    return jnp.where(lane < 64, top, total), scales


def pack_tile(tile):
    high = tile.astype(BF16).astype(F32)
    return jnp.concatenate([high, tile - high], 0).astype(BF16)


def unpack_tile(rows):
    rows = rows.astype(F32)
    return rows[:8] + rows[8:]


def scale_rows(scale, rows):
    n = rows.shape[0] // 8
    return jnp.concatenate([lane_bcast(scale, k) * rows[8 * k : 8 * k + 8] for k in range(n)], 0)


def kernel(
    q_hbm, root_hbm, doc_hbm, suf_hbm, new_hbm, len_hbm, rd_hbm, ol_hbm, dr_hbm,
    out_ref,
    qbuf, raw, f32s, keys, vals, suf, newb, newf, tail_s, len_s, rd_s, ol_s, dr_s,
    ns1, nr1, own2, ss2, ns2, nr2, ns3, nr3,
    tail_num, tail_m, tail_l,
    lsem, kvs, kvr, zs, zr, bs, br_, as_, ar_, r1s, r1r, r2s, r2r, r3s, r3r,
):
    me = lax.axis_index("seq")
    core = lax.rem(me, 2)
    z = lax.rem(me // 2, 4)
    y = lax.rem(me // 8, 4)
    x = me // 32

    def dev(xx, yy, zz, cc):
        return {"seq": ((xx * 4 + yy) * 4 + zz) * 2 + cc}

    def zpeer(d, c):
        return dev(x, y, lax.rem(z + d, 4), c)

    def xpeer(d, c):
        return dev(lax.rem(x + d, 4), y, z, c)

    def ypeer(d, c):
        return dev(x, lax.rem(y + d, 4), z, c)

    def along(x_step, y_step, c):
        return dev(lax.rem(x + x_step, 4), lax.rem(y + y_step, 4), z, c)

    apeer = (xpeer, ypeer)
    bpeer = (ypeer, xpeer)
    partner = dev(x, y, z, 1 - core)

    local = []

    def fetch(src, dst):
        c = pltpu.make_async_copy(src, dst, lsem.at[len(local)])
        c.start()
        local.append(c)
        return c

    c_q = fetch(q_hbm, qbuf.at[0, 0, 0, 0])
    c_root = fetch(root_hbm, raw.at[0, 0])
    c_doc = fetch(doc_hbm, raw.at[1, 0])
    c_ol = fetch(ol_hbm, ol_s)
    c_rd = fetch(rd_hbm, rd_s)
    c_dr = fetch(dr_hbm, dr_s)
    c_len = fetch(len_hbm, len_s)
    c_new = fetch(new_hbm, newb)
    c_suf = fetch(suf_hbm, suf)

    barrier = pltpu.get_barrier_semaphore()
    axes = [(f, d) for f in (xpeer, ypeer, zpeer) for d in (1, 2, 3)]
    peers = [partner] + [f(d, c) for f, d in axes for c in (core, 1 - core)]
    for p in peers:
        pl.semaphore_signal(barrier, inc=1, device_id=p, device_id_type=pl.DeviceIdType.MESH)
    pl.semaphore_wait(barrier, len(peers))

    def send(src, dst, ss, rs, to):
        c = pltpu.make_async_remote_copy(
            src_ref=src, dst_ref=dst, send_sem=ss, recv_sem=rs,
            device_id=to, device_id_type=pl.DeviceIdType.MESH,
        )
        c.start()
        return c

    def wait_for(ref, sem):
        pltpu.make_async_copy(ref, ref, sem).wait()

    sent = []

    def to_b(path, zz):
        for d in (3, 2, 1):
            r = 4 - d
            sent.append(send(qbuf.at[path, 0, 0, zz], qbuf.at[path, 0, r, zz], bs.at[path, d - 1, zz], br_.at[path, r - 1, zz], bpeer[path](d, core)))

    def to_a(path):
        for d in (3, 2, 1):
            r = 4 - d
            sent.append(send(qbuf.at[path, 0, 0], qbuf.at[path, r, 0], as_.at[path, d - 1, 0], ar_.at[path, r - 1, 0], apeer[path](d, core)))

    def on_to_a(path, d):
        r = 4 - d
        sent.append(send(qbuf.at[path, 0, pl.ds(1, 3)], qbuf.at[path, r, pl.ds(1, 3)], as_.at[path, d - 1, 1], ar_.at[path, r - 1, 1], apeer[path](d, core)))

    c_q.wait()
    for d in (3, 2, 1):
        r = 4 - d
        sent.append(send(qbuf.at[0, 0, 0, 0], qbuf.at[r // 2, 0, 0, r % 2], zs.at[d - 1], zr.at[r - 1], zpeer(d, core)))
    to_b(0, 0)
    kv_root = send(root_hbm, raw.at[0, 1], kvs.at[0], kvr.at[0], partner)
    kv_doc = send(doc_hbm, raw.at[1, 1], kvs.at[1], kvr.at[1], partner)

    vals[:, :, HD:] = jnp.ones((2, 1024, HD), BF16)
    newf[...] = jnp.zeros_like(newf)

    def split_heads(src, who):
        for kv in range(2):
            f32s[src, who, kv] = raw[src, who, kv].astype(F32)
            base = src * 512 + who * 256
            for h in range(2):
                part = f32s[src, who, kv, pl.ds(h, 256, stride=2), :].astype(BF16)
                if kv == 0:
                    keys[h, base : base + 256] = part
                else:
                    vals[h, base : base + 256, :HD] = part

    c_root.wait()
    split_heads(0, 0)
    c_doc.wait()
    split_heads(1, 0)

    for r in (1, 3, 2):
        path, zz = r // 2, r % 2
        wait_for(qbuf.at[path, 0, 0, zz], zr.at[r - 1])
        to_b(path, zz)
    for path in range(2):
        to_a(path)

    kv_root.wait_recv()
    split_heads(0, 1)
    kv_doc.wait_recv()
    split_heads(1, 1)

    for d in (3, 2, 1):
        for path in range(2):
            if d == 3:
                for r in (1, 3, 2):
                    for zz in range(2):
                        wait_for(qbuf.at[path, 0, r, zz], br_.at[path, r - 1, zz])
            on_to_a(path, d)

    for c in (c_ol, c_rd, c_dr, c_len, c_new, c_suf):
        c.wait()
    length = len_s[0]
    qown = qbuf[0, 0, 0, 0]
    row = lax.broadcasted_iota(jnp.int32, (ROWS, 1024), 0)
    col = lax.broadcasted_iota(jnp.int32, (ROWS, 1024), 1)
    same = (row // 8) % 2 == col % 2
    tops = []
    for c in range(4):
        s = lax.dot_general(qown, suf[0, 1024 * c : 1024 * c + 1024], NT, preferred_element_type=F32)
        s = jnp.where(same & (col // 2 < length - 512 * c), s, -BIG)
        tail_s[:, 1024 * c : 1024 * c + 1024] = s
        tops.append(jnp.max(s, 1, keepdims=True))
    for kv in range(2):
        for j in range(3):
            newf[kv, 2 * j : 2 * j + 2] = newb[kv, j].astype(F32)
    s_new = lax.dot_general(qown, newf[0].astype(BF16), NT, preferred_element_type=F32)
    r128, c128 = row[:, :128], col[:, :128]
    s_new = jnp.where(((r128 // 8) % 2 == c128 % 2) & (c128 // 2 <= r128 // 16) & (c128 < 6), s_new, -BIG)
    tops.append(jnp.max(s_new, 1, keepdims=True))
    top = functools.reduce(jnp.maximum, tops)
    p_new = jnp.exp2((s_new - top) * COEF).astype(BF16)
    num = lax.dot_general(p_new, newf[1].astype(BF16), (((1,), (0,)), ((), ())), preferred_element_type=F32)
    total = jnp.sum(p_new.astype(F32), 1, keepdims=True)
    for c in range(4):
        p = jnp.exp2((tail_s[:, 1024 * c : 1024 * c + 1024] - top) * COEF).astype(BF16)
        num += jnp.dot(p, suf[1, 1024 * c : 1024 * c + 1024], preferred_element_type=F32)
        total += jnp.sum(p.astype(F32), 1, keepdims=True)
    tail_num[...] = num
    tail_m[...] = jnp.broadcast_to(top, (ROWS, 128))
    tail_l[...] = jnp.broadcast_to(total, (ROWS, 128))

    lane = lax.broadcasted_iota(jnp.int32, (8, 128), 1)
    chip = me // 2

    def block(a_rel):
        q = qbuf[:, a_rel].reshape(16 * ROWS, HD).astype(F32).reshape(48, 2, 8, HD)
        bars = []
        for path in range(2):
            for b_rel in range(4):
                xx = lax.rem(x + (b_rel if path else a_rel), 4)
                yy = lax.rem(y + (a_rel if path else b_rel), 4)
                for zz in range(2):
                    slot = ((xx * 4 + yy) * 4 + lax.rem(z + 2 * path + zz, 4)) * 2 + core
                    run = dr_s[rd_s[ol_s[slot]]]
                    bars.append(jnp.full((24, 1), jnp.where(run == chip, 0.0, BIG), F32))
        bar = jnp.concatenate(bars, 0)
        nums, tiles = [], [jnp.zeros((8, 128), F32)] * 2
        for h in range(2):
            qh = q[:, h].reshape(48 * 8, HD).astype(BF16)
            s = lax.dot_general(qh, keys[h], NT, preferred_element_type=F32)
            s0, s1 = s[:, :512], s[:, 512:]
            m = jnp.maximum(jnp.max(s0, 1, keepdims=True), jnp.max(s1, 1, keepdims=True) - bar)
            m = m.astype(BF16).astype(F32)
            p0 = jnp.exp2((s0 - m) * COEF).astype(BF16)
            p1 = jnp.exp2((s1 - (m + bar)) * COEF).astype(BF16)
            o = jnp.dot(jnp.concatenate([p0, p1], 1), vals[h], preferred_element_type=F32)
            nums.append(o[:, :HD].reshape(48, 1, 8, HD))
            for i in range(48):
                k = 2 * (i % 24) + h
                tile = jnp.where(lane == k, m[8 * i : 8 * i + 8], tiles[i // 24])
                tiles[i // 24] = jnp.where(lane == 64 + k, o[8 * i : 8 * i + 8, HD:], tile)
        ns1[:, a_rel, : 8 * ROWS] = jnp.concatenate(nums, 1).reshape(2, 8 * ROWS, HD).astype(BF16)
        for path in range(2):
            ns1[path, a_rel, 8 * ROWS :] = pack_tile(tiles[path])

    def rs1(path, d):
        r = lax.rem(4 - d, 4)
        to = along(jnp.where(path == 0, d, 0), jnp.where(path == 0, 0, d), 1)
        return pltpu.make_async_remote_copy(
            src_ref=ns1.at[path, d], dst_ref=nr1.at[core, path, r], send_sem=r1s.at[path, d],
            recv_sem=r1r.at[core, path, r], device_id=to, device_id_type=pl.DeviceIdType.MESH)

    def step(a_rel, carry):
        @pl.when(a_rel > 0)
        def _():
            for path in range(2):
                wait_for(qbuf.at[path, a_rel, 0], ar_.at[path, a_rel - 1, 0])
                wait_for(qbuf.at[path, a_rel, pl.ds(1, 3)], ar_.at[path, a_rel - 1, 1])

        block(a_rel)

        @pl.when((a_rel > 0) | (core == 0))
        def _():
            for path in range(2):
                rs1(path, a_rel).start()

        @pl.when((a_rel == 0) & (core == 1))
        def _():
            for path in range(2):
                pltpu.make_async_copy(ns1.at[path, 0], nr1.at[1, path, 0], r1r.at[1, path, 0]).start()

        return carry

    lax.fori_loop(0, 4, step, 0)

    def rs2(plane, path, d):
        r = 4 - d
        to = along(jnp.where(path == 0, 0, d), jnp.where(path == 0, d, 0), 1)
        return pltpu.make_async_remote_copy(
            src_ref=ns2.at[plane, path, d - 1], dst_ref=nr2.at[plane, path, r - 1], send_sem=r2s.at[plane, path, d - 1],
            recv_sem=r2r.at[plane, path, r - 1], device_id=to, device_id_type=pl.DeviceIdType.MESH)

    def rs3(plane, path, zz):
        d = 2 * path + zz
        r = lax.rem(4 - d, 4)
        return pltpu.make_async_remote_copy(
            src_ref=ns3.at[plane, d], dst_ref=nr3.at[r], send_sem=r3s.at[plane, d], recv_sem=r3r.at[r],
            device_id=zpeer(d, plane), device_id_type=pl.DeviceIdType.MESH)

    def back_a(i, carry):
        plane, path = 1 - lax.rem(i, 2), i // 2
        for r in (0, 3, 2, 1):
            wait_for(nr1.at[plane, path, r], r1r.at[plane, path, r])
        msgs = [nr1.at[plane, path, r] for r in range(4)]
        tile, scales = merge_tiles([unpack_tile(p[8 * ROWS :]) for p in msgs])
        acc = sum(scale_rows(e, p[: 8 * ROWS].astype(F32)) for e, p in zip(scales, msgs))
        own2[plane, path] = acc[:96]
        ss2[plane, path] = tile
        for d in (2, 1, 3):
            ns2[plane, path, d - 1, :96] = acc[96 * d : 96 * (d + 1)].astype(BF16)
            ns2[plane, path, d - 1, 96:] = pack_tile(tile)
        for d in (2, 1, 3):
            rs2(plane, path, d).start()
        return carry

    def back_b(i, carry):
        plane, path = 1 - lax.rem(i, 2), i // 2
        for r in (1, 3, 2):
            wait_for(nr2.at[plane, path, r - 1], r2r.at[plane, path, r - 1])
        tiles = [ss2[plane, path]]
        tiles += [pltpu.roll(unpack_tile(nr2[plane, path, r - 1, 96:]), 128 - 12 * (4 - r), 1) for r in (1, 2, 3)]
        tile, scales = merge_tiles(tiles)
        acc = scale_rows(scales[0], own2[plane, path])
        for r in range(3):
            acc += scale_rows(scales[r + 1], nr2[plane, path, r, :96].astype(F32))
        for zz in range(2):
            ns3[plane, 2 * path + zz, :ROWS] = acc[ROWS * zz : ROWS * zz + ROWS].astype(BF16)
            ns3[plane, 2 * path + zz, ROWS:] = pack_tile(tile)
        here = (plane == 1) & (path == 0)

        @pl.when(jnp.logical_not(here))
        def _():
            rs3(plane, path, 0).start()

        @pl.when(here)
        def _():
            pltpu.make_async_copy(ns3.at[1, 0], nr3.at[0], r3r.at[0]).start()

        rs3(plane, path, 1).start()
        return carry

    @pl.when(core == 1)
    def _():
        lax.fori_loop(0, 4, back_a, 0)
        lax.fori_loop(0, 4, back_b, 0)

    for r in (0, 3, 1, 2):
        wait_for(nr3.at[r], r3r.at[r])
    parts = []
    for r in range(4):
        t = unpack_tile(nr3[r, ROWS:])
        parts.append((nr3[r, :ROWS].astype(F32), pltpu.roll(t, 128 - 6, 1) if r % 2 else t))
    for k in range(6):
        at = slice(8 * k, 8 * k + 8)
        tops = [lane_bcast(t, k) for _, t in parts] + [tail_m[at]]
        sums = [lane_bcast(t, 64 + k) for _, t in parts] + [tail_l[at]]
        nums = [n[at] for n, _ in parts] + [tail_num[at]]
        top = functools.reduce(jnp.maximum, tops)
        es = [jnp.exp2((t - top) * COEF) for t in tops]
        den = sum(e * s for e, s in zip(es, sums))
        res = sum(e * v for e, v in zip(es, nums)) / den
        for g in range(8):
            col = (8 * (k % 2) + g) * HD
            out_ref[0, k // 2 : k // 2 + 1, col : col + HD] = res[g : g + 1].astype(BF16)

    kv_root.wait_send()
    kv_doc.wait_send()
    for path in range(2):
        for d in (1, 2, 3):
            wait_for(ns1.at[path, d], r1s.at[path, d])

    for c in sent:
        c.wait_send()

    @pl.when(core == 0)
    def _():
        for path in range(2):
            wait_for(ns1.at[path, 0], r1s.at[path, 0])

    @pl.when(core == 1)
    def _():
        for plane in range(2):
            for path in range(2):
                for d in (1, 2, 3):
                    wait_for(ns2.at[plane, path, d - 1], r2s.at[plane, path, d - 1])
            for d in range(4):
                if (plane, d) != (1, 0):
                    wait_for(ns3.at[plane, d], r3s.at[plane, d])


def body(queries, root_kv, doc_kv, suffix_kv, new_kv, suffix_len, request_doc, owner_list, doc_run):
    vm, dma = pltpu.VMEM, pltpu.SemaphoreType.DMA
    any_spec = pl.BlockSpec(memory_space=pltpu.HBM)
    out = pl.pallas_call(
        kernel,
        out_shape=pltpu.VMEM((1, 3, 2048), BF16),
        in_specs=[any_spec] * 9,
        out_specs=pl.BlockSpec(memory_space=pltpu.VMEM),
        scratch_shapes=[
            vm((2, 4, 4, 2, ROWS, HD), BF16),
            vm((2, 2, 2, 512, HD), BF16),
            vm((2, 2, 2, 512, HD), F32),
            vm((2, 1024, HD), BF16),
            vm((2, 1024, 2 * HD), BF16),
            vm((2, 4096, HD), BF16),
            vm((2, 3, 2, HD), BF16),
            vm((2, 128, HD), F32),
            vm((ROWS, 4096), F32),
            pltpu.SMEM((1,), jnp.int32),
            pltpu.SMEM((128,), jnp.int32),
            pltpu.SMEM((128,), jnp.int32),
            pltpu.SMEM((64,), jnp.int32),
            vm((2, 4, 8 * ROWS + 16, HD), BF16),
            vm((2, 2, 4, 8 * ROWS + 16, HD), BF16),
            vm((2, 2, 96, HD), F32),
            vm((2, 2, 8, 128), F32),
            vm((2, 2, 3, 112, HD), BF16),
            vm((2, 2, 3, 112, HD), BF16),
            vm((2, 4, 64, HD), BF16),
            vm((4, 64, HD), BF16),
            vm((ROWS, HD), F32),
            vm((ROWS, HD), F32),
            vm((ROWS, HD), F32),
            dma((9,)),
            dma((2,)), dma((2,)),
            dma((3,)), dma((3,)),
            dma((2, 3, 2)), dma((2, 3, 2)),
            dma((2, 3, 2)), dma((2, 3, 2)),
            dma((2, 4)), dma((2, 2, 4)),
            dma((2, 2, 3)), dma((2, 2, 3)),
            dma((2, 4)), dma((4,)),
        ],
        compiler_params=pltpu.CompilerParams(
            collective_id=0, has_side_effects=True, vmem_limit_bytes=60 * 1024 * 1024
        ),
    )(
        queries.reshape(ROWS, HD),
        root_kv.reshape(2, 512, HD),
        doc_kv.reshape(2, 512, HD),
        suffix_kv.reshape(2, 4096, HD),
        new_kv.reshape(2, 3, 2, HD),
        suffix_len,
        request_doc.reshape(128),
        owner_list,
        doc_run,
    )
    return out


def solution(mesh):
    in_specs = (
        P("seq", None, "kvh", None, None),
        P(None, "seq", "kvh", None),
        P(None, "seq", "kvh", None),
        P(None, "seq", None, "kvh", None),
        P(None, "seq", None, "kvh", None),
        P("seq"),
        P(),
        P(),
        P(),
    )
    out_specs = P("seq", None, "kvh")
    return jax.shard_map(body, mesh=mesh, in_specs=in_specs, out_specs=out_specs, check_vma=False)
```
